32 devices in a mesh: frames: 4 (over y, x), modes: 8 (over z, core).
Axes of the slice: x: 2, y: 2, z: 4, core: 2. Of those that a mesh axis runs over, the one named last changes fastest.
Arguments:
- momentum: bfloat16 [16, 512, 512, 256], P('frames', 'modes'), may hold values from -6 to 6
- ky_list: int32 [192], replicated, may hold values from 0 to 511, as said below
- kx_list: int32 [8], replicated, may hold values from 0 to 511, as said below
- ky_gain: float32 [192], replicated, may hold values from 0.5 to 2
- kx_gain: float32 [8], replicated, may hold values from 0.5 to 2
- pair_first: int32 [8], replicated, may hold values from 0 to 3
- pair_second: int32 [8], replicated, may hold values from 0 to 3
Outputs:
- correlation: float32 [192, 8, 2, 256, 256], P('modes', 'frames')
The draws below stay inside these ranges and needn't reach their ends.
Inputs may be any that keep to these rules, and one draw needn't show every extreme that they name: `ky_list`: 192 distinct wavenumbers. `kx_list`: 8 distinct wavenumbers.
All inputs are finite; a program needn't handle non-finite values.
Results may differ from the reference program's by a relative error of at most 0.014.
Values may be sent and summed in bfloat16 or wider, within the bound.
A program may use at most 320 MiB of HBM per device.

```python
import math
import jax
import jax.numpy as jnp
from jax import lax

NX = 512
NY = 512
NZ = 256
KY = 192
KX = 8
FR_DEV = 4
NPAIR = 8
FRAMES = 16


def pick_distinct(key, total, wanted):
    first_key, second_key = jax.random.split(key)
    middle = jax.random.permutation(first_key, jnp.arange(1, total - 1, dtype=jnp.int32))[:wanted - 2]
    chosen = jnp.concatenate([jnp.array([0, total - 1], dtype=jnp.int32), middle])
    return jax.random.permutation(second_key, chosen)


def draw_ky_list(key, part):
    key = jax.random.fold_in(key, 11)
    return pick_distinct(key, NY, KY)


def draw_kx_list(key, part):
    key = jax.random.fold_in(key, 17)
    return pick_distinct(key, NX, KX)


def draw_pair_first(key, part):
    key = jax.random.fold_in(key, 31)
    values = jax.random.randint(key, (NPAIR,), 0, FR_DEV, dtype=jnp.int32)
    return values.at[0].set(0).at[1].set(FR_DEV - 1)


def draw_pair_second(key, part):
    key = jax.random.fold_in(key, 37)
    values = jax.random.randint(key, (NPAIR,), 0, FR_DEV, dtype=jnp.int32)
    return values.at[0].set(FR_DEV - 1).at[1].set(0)


def level_of(stream_key, dims, shards, least, largest):
    gain, own = 1.0, jax.random.fold_in(stream_key, 6)
    for axis_at, shards_of in shards:
        heights = jnp.exp(jax.random.uniform(jax.random.fold_in(own, axis_at), (shards_of,), jnp.float32, least / len(shards), largest / len(shards)))
        gain = gain * jnp.repeat(heights, dims[axis_at] // shards_of).reshape([-1 if axis == axis_at else 1 for axis in range(len(dims))])
    return gain


def gaussian(key, shape, width, most, shards=(), kind=jnp.bfloat16):
    level = level_of(key, shape, shards, -0.22, 0.18) if shards else 1.0
    values = jax.random.normal(key, shape, jnp.float32) * width * level
    return jnp.minimum(jnp.maximum(values, -most), most).astype(kind)


def setup_inputs(seed: int = 0) -> dict:
    splits = jax.random.split(jax.random.key(seed), 8)
    return {
        "momentum": gaussian(splits[0], (FRAMES, NX, NY, NZ), 1.0, 6.0, ((0, 4), (1, 8))),
        "ky_list": draw_ky_list(jax.random.fold_in(splits[7], 71), 0),
        "kx_list": draw_kx_list(jax.random.fold_in(splits[7], 71), 0),
        "ky_gain": jnp.clip(jnp.exp(jax.random.uniform(splits[3], (KY,), jnp.float32, math.log(0.5), math.log(2.0))), 0.5, 2.0),
        "kx_gain": jnp.clip(jnp.exp(jax.random.uniform(splits[4], (KX,), jnp.float32, math.log(0.5), math.log(2.0))), 0.5, 2.0),
        "pair_first": draw_pair_first(jax.random.fold_in(splits[7], 71), 0),
        "pair_second": draw_pair_second(jax.random.fold_in(splits[7], 71), 0),
    }


def tables(ky_list, kx_list, ky_gain, kx_gain, grid_x, grid_y):
    y_index = jnp.arange(grid_y, dtype=jnp.int32)
    phase_y = (y_index[:, None] * ky_list[None, :] % grid_y).astype(jnp.float32) * (2.0 * math.pi / grid_y)
    y_scale = ky_gain[None, :] / math.sqrt(grid_y)
    y_table = jnp.stack([jnp.cos(phase_y) * y_scale, -jnp.sin(phase_y) * y_scale], axis=2)
    y_table = y_table.reshape(grid_y, 2 * ky_list.shape[0]).astype(jnp.bfloat16)
    x_index = jnp.arange(grid_x, dtype=jnp.int32)
    phase_x = (x_index[:, None] * kx_list[None, :] % grid_x).astype(jnp.float32) * (2.0 * math.pi / grid_x)
    x_scale = kx_gain[None, :] / math.sqrt(grid_x)
    x_table = jnp.concatenate([jnp.cos(phase_x) * x_scale, jnp.sin(phase_x) * x_scale], axis=1).astype(jnp.bfloat16)
    return (y_table, x_table)

def combine(column_sums):
    frame_count, col_count, mode_count, cell_count = column_sums.shape
    parted = column_sums.reshape(frame_count, col_count // 2, 2, 2, mode_count // 2, cell_count)
    real_part = parted[:, :, 0, 0] + parted[:, :, 1, 1]
    imag_part = parted[:, :, 1, 0] - parted[:, :, 0, 1]
    return jnp.stack([real_part, imag_part], axis=3)

def reference(momentum, ky_list, kx_list, ky_gain, kx_gain, pair_first, pair_second):
    high = lax.Precision.HIGHEST
    y_table, x_table = tables(ky_list, kx_list, ky_gain, kx_gain, NX, NY)

    def single_frame(frame_data):
        planes = jnp.einsum('xyz,yc->xcz', frame_data.astype(jnp.float32), y_table.astype(jnp.float32), precision=high).astype(jnp.bfloat16)
        column_sums = jnp.einsum('xcz,xk->ckz', planes.astype(jnp.float32), x_table.astype(jnp.float32), precision=high)
        return combine(column_sums[None])[0]
    modal = lax.map(single_frame, momentum)
    frame_mean = lax.optimization_barrier(jnp.sum(modal, axis=0)) / FRAMES
    centered = modal - frame_mean
    offsets = jnp.arange(FR_DEV, dtype=jnp.int32)
    first_hot = (pair_first[:, None] == offsets[None, :]).astype(jnp.float32)
    second_hot = (pair_second[:, None] == offsets[None, :]).astype(jnp.float32)
    counts = jnp.dot(first_hot.T, second_hot, precision=high)
    pair_total = pair_first.shape[0]
    blocks = centered.reshape(FRAMES // FR_DEV, FR_DEV, KY, KX, 2, NZ)

    def one_wave(coeffs):
        weighted = jnp.einsum('ab,nakrz->nbkrz', counts, coeffs, precision=high)
        turned = jnp.stack([coeffs[:, :, :, 1], -coeffs[:, :, :, 0]], axis=3)
        real_corr = jnp.einsum('nbkrz,nbkry->nkzy', weighted, coeffs, precision=high)
        imag_corr = jnp.einsum('nbkrz,nbkry->nkzy', weighted, turned, precision=high)
        block_corr = jnp.stack([real_corr, imag_corr], axis=2) / pair_total
        rounded = lax.optimization_barrier(block_corr.astype(jnp.bfloat16)).astype(jnp.float32)
        return lax.optimization_barrier(jnp.sum(rounded, axis=0))
    return lax.map(one_wave, jnp.moveaxis(blocks, 2, 0))
```

```python
import functools
import math

import jax
import jax.numpy as jnp
from jax import lax
from jax.experimental import pallas as pl
from jax.experimental.pallas import tpu as pltpu
from jax.sharding import PartitionSpec as P

MESH = pl.DeviceIdType.MESH
ROWS = 16
CHUNK = 64
SLOTS = 3


def wave_tables(ky_list, kx_list, ky_gain, kx_gain, x_index, grid_x, grid_y):
    y_index = jnp.arange(grid_y, dtype=jnp.int32)
    phase_y = (ky_list[:, None] * y_index[None, :] % grid_y).astype(jnp.float32) * (
        2.0 * math.pi / grid_y
    )
    y_scale = ky_gain[:, None] / math.sqrt(grid_y)
    y_cos = (jnp.cos(phase_y) * y_scale).astype(jnp.bfloat16)
    y_sin = (-jnp.sin(phase_y) * y_scale).astype(jnp.bfloat16)
    phase_x = (kx_list[:, None] * x_index[None, :] % grid_x).astype(jnp.float32) * (
        2.0 * math.pi / grid_x
    )
    x_scale = kx_gain[:, None] / math.sqrt(grid_x)
    x_cos = (jnp.cos(phase_x) * x_scale).astype(jnp.bfloat16)
    x_sin = (jnp.sin(phase_x) * x_scale).astype(jnp.bfloat16)
    return y_cos, y_sin, x_cos, x_sin


def pair_counts(pair_first, pair_second, block_len):
    offsets = jnp.arange(block_len, dtype=jnp.int32)
    first_hot = pair_first[:, None, None] == offsets[None, :, None]
    second_hot = pair_second[:, None, None] == offsets[None, None, :]
    return jnp.sum((first_hot & second_hot).astype(jnp.float32), axis=0)


def modal_kernel(
    groups, half, share,
    counts_ref, m_ref, w_ref, a_ref, z_ref,
    mbuf, ghi, glo, own, partner, outgoing, landed,
    m_sem, pair_send, pair_recv, send_sem, recv_sem,
):
    frames, _, grid_y, cells = m_ref.shape
    rows = a_ref.shape[0] // (2 * half)
    waves = groups * share
    fr = lax.axis_index("frames")
    mode = lax.axis_index("modes")
    core = lax.rem(mode, 2)
    line = lax.div(mode, 2)
    me = fr * half + line
    peers = groups * half
    other = (fr, line * 2 + 1 - core)
    chunks = grid_y // CHUNK

    def peer_at(step):
        at = lax.rem(me + step, peers)
        return at, lax.div(at, half), lax.rem(at, half)

    barrier = pltpu.get_barrier_semaphore()

    def greet(step, carry):
        _, f, l = peer_at(step)
        pl.semaphore_signal(barrier, inc=1, device_id=(f, l * 2 + core), device_id_type=MESH)
        return carry

    def load(index):
        slot = lax.rem(index, SLOTS)
        start = pl.multiple_of(lax.rem(index, chunks) * CHUNK, CHUNK)
        return pltpu.make_async_copy(
            m_ref.at[lax.div(index, chunks), :, pl.ds(start, CHUNK), :],
            mbuf.at[slot], m_sem.at[slot],
        )

    for index in range(SLOTS - 1):
        load(jnp.int32(index)).start()
    lax.fori_loop(1, peers, greet, 0)
    pl.semaphore_signal(barrier, inc=1, device_id=other, device_id_type=MESH)
    pl.semaphore_wait(barrier, peers)

    def x_chunk(t, c, carry):
        index = t * chunks + c
        load(index).wait()

        @pl.when(index + SLOTS - 1 < frames * chunks)
        def _():
            load(index + SLOTS - 1).start()

        slot = lax.rem(index, SLOTS)
        for g in range(CHUNK // ROWS):
            block = mbuf[slot, :, g * ROWS:(g + 1) * ROWS, :]
            part = jnp.dot(
                w_ref[...], block.reshape(-1, cells), preferred_element_type=jnp.float32
            )
            high = part.astype(jnp.bfloat16)
            low = (part - high.astype(jnp.float32)).astype(jnp.bfloat16)
            at = pl.ds(pl.multiple_of(c * CHUNK + g * ROWS, ROWS), ROWS)
            ghi[:, at, :] = high.reshape(2 * waves, ROWS, cells)
            glo[:, at, :] = low.reshape(2 * waves, ROWS, cells)
        return carry

    def y_wave(t, k, carry):
        f, kk = lax.div(k, share), lax.rem(k, share)
        pair = pl.ds(2 * k, 2)
        total = jnp.dot(
            a_ref[...], ghi[pair].reshape(2 * grid_y, cells), preferred_element_type=jnp.float32
        ) + jnp.dot(
            a_ref[...], glo[pair].reshape(2 * grid_y, cells), preferred_element_type=jnp.float32
        )
        own[t, :, f, kk] = total.reshape(2, half * rows, cells).astype(jnp.bfloat16)
        return carry

    def pair_copy(t):
        return pltpu.make_async_remote_copy(
            src_ref=own.at[t, 1 - core], dst_ref=partner.at[t],
            send_sem=pair_send.at[t], recv_sem=pair_recv.at[t],
            device_id=other, device_id_type=MESH,
        )

    def spread(t):
        pair_copy(t).wait()

        def add(k, carry):
            f, kk = lax.div(k, share), lax.rem(k, share)
            total = own[t, core, f, kk].astype(jnp.float32) + partner[t, f, kk].astype(jnp.float32)
            outgoing[t, f, :, kk] = total.astype(jnp.bfloat16).reshape(half, rows, cells)
            return carry

        lax.fori_loop(0, waves, add, 0)

        def send(step, carry):
            at, f, l = peer_at(step)
            pltpu.make_async_remote_copy(
                src_ref=outgoing.at[t, f, l], dst_ref=landed.at[fr, line, t],
                send_sem=send_sem.at[at], recv_sem=recv_sem.at[me],
                device_id=(f, l * 2 + core), device_id_type=MESH,
            ).start()
            return carry

        lax.fori_loop(1, peers, send, 0)
        landed[fr, line, t] = outgoing[t, fr, line]

    def frame(t, carry):
        lax.fori_loop(0, 1, functools.partial(x_chunk, t), 0)

        @pl.when(t > 0)
        def _():
            spread(t - 1)

        lax.fori_loop(1, chunks, functools.partial(x_chunk, t), 0)
        lax.fori_loop(0, waves, functools.partial(y_wave, t), 0)
        pair_copy(t).start()
        return carry

    lax.fori_loop(0, frames, frame, 0)
    spread(jnp.int32(frames - 1))

    def collect(step, carry):
        at, f, l = peer_at(step)
        pltpu.make_async_remote_copy(
            src_ref=outgoing.at[:, f, l], dst_ref=landed.at[f, l],
            send_sem=send_sem.at[at], recv_sem=recv_sem.at[at],
            device_id=(f, l * 2 + core), device_id_type=MESH,
        ).wait()
        return carry

    lax.fori_loop(1, peers, collect, 0)

    def finish(index, carry):
        kk = lax.div(index, rows // ROWS)
        at = pl.ds(pl.multiple_of(lax.rem(index, rows // ROWS) * ROWS, ROWS), ROWS)
        modal = [
            [
                jnp.sum(landed[f, :, t, kk, at, :].astype(jnp.float32), axis=0)
                for t in range(frames)
            ]
            for f in range(groups)
        ]
        mean = sum(value for block in modal for value in block) / (groups * frames)
        for f in range(groups):
            centered = [value - mean for value in modal[f]]
            for b in range(frames):
                weighted = sum(counts_ref[a, b] * centered[a] for a in range(frames))
                for first, value in ((0, weighted), (2, centered[b])):
                    high = value.astype(jnp.bfloat16)
                    low = (value - high.astype(jnp.float32)).astype(jnp.bfloat16)
                    z_ref[first, f * frames + b, kk, at, :] = high
                    z_ref[first + 1, f * frames + b, kk, at, :] = low
        return carry

    lax.fori_loop(0, share * (rows // ROWS), finish, 0)


def corr_kernel(z_ref, out_ref):
    share, _, depth, _ = z_ref.shape[1:]
    mid = depth // 2
    for kk in range(share):
        left = jnp.concatenate([z_ref[0, kk, 0], z_ref[0, kk, 1], z_ref[0, kk, 0]], axis=0)
        high, low = z_ref[0, kk, 2], z_ref[0, kk, 3]
        right = jnp.concatenate([high, high, low], axis=0)
        turned = [jnp.concatenate([v[mid:], -v[:mid]], axis=0) for v in (high, low)]
        turned = jnp.concatenate([turned[0], turned[0], turned[1]], axis=0)
        dims = (((0,), (0,)), ((), ()))
        out_ref[0, kk, 0] = lax.dot_general(left, right, dims, preferred_element_type=jnp.float32)
        out_ref[0, kk, 1] = lax.dot_general(left, turned, dims, preferred_element_type=jnp.float32)


def per_device(momentum, ky_list, kx_list, ky_gain, kx_gain, pair_first, pair_second):
    frames, row_share, grid_y, cells = momentum.shape
    groups, modes = lax.axis_size("frames"), lax.axis_size("modes")
    half = modes // 2
    wave_y, wave_x = ky_list.shape[0], kx_list.shape[0]
    per_y, share = wave_y // modes, wave_x // groups
    rows = -(-2 * per_y // ROWS) * ROWS
    x_index = lax.axis_index("modes") * row_share + jnp.arange(row_share, dtype=jnp.int32)
    y_cos, y_sin, x_cos, x_sin = wave_tables(
        ky_list, kx_list, ky_gain, kx_gain, x_index, row_share * modes, grid_y
    )
    upper = jnp.concatenate([y_cos, y_sin], axis=1)
    lower = jnp.concatenate([y_sin, -y_cos], axis=1)
    table = jnp.stack([upper, lower]).reshape(2, half, 2, per_y, 2 * grid_y)
    table = table.transpose(2, 1, 0, 3, 4).reshape(2, half, 2 * per_y, 2 * grid_y)
    table = jnp.pad(table, ((0, 0), (0, 0), (0, rows - 2 * per_y), (0, 0)))
    table = table.reshape(2 * half * rows, 2 * grid_y)
    x_rows = jnp.stack([x_cos, x_sin], axis=1).reshape(2 * wave_x, row_share)
    x_wide = jnp.repeat(jnp.repeat(x_rows, ROWS, axis=1), ROWS, axis=0)
    same = (
        lax.broadcasted_iota(jnp.int32, x_wide.shape, 0) % ROWS
        == lax.broadcasted_iota(jnp.int32, x_wide.shape, 1) % ROWS
    )
    spread_x = jnp.where(same, x_wide, jnp.zeros_like(x_wide))
    counts = pair_counts(pair_first, pair_second, frames) / pair_first.shape[0]

    bf16 = jnp.bfloat16
    vmem = pl.BlockSpec(memory_space=pltpu.VMEM)
    peers = groups * half
    parts = pl.pallas_call(
        functools.partial(modal_kernel, groups, half, share),
        out_shape=jax.ShapeDtypeStruct((4, groups * frames, share, rows, cells), bf16),
        in_specs=[
            pl.BlockSpec(memory_space=pltpu.SMEM),
            pl.BlockSpec(memory_space=pl.ANY),
            vmem,
            vmem,
        ],
        out_specs=vmem,
        scratch_shapes=[
            pltpu.VMEM((SLOTS, row_share, CHUNK, cells), bf16),
            pltpu.VMEM((2 * wave_x, grid_y, cells), bf16),
            pltpu.VMEM((2 * wave_x, grid_y, cells), bf16),
            pltpu.VMEM((frames, 2, groups, share, half * rows, cells), bf16),
            pltpu.VMEM((frames, groups, share, half * rows, cells), bf16),
            pltpu.VMEM((frames, groups, half, share, rows, cells), bf16),
            pltpu.VMEM((groups, half, frames, share, rows, cells), bf16),
            pltpu.SemaphoreType.DMA((SLOTS,)),
            pltpu.SemaphoreType.DMA((frames,)),
            pltpu.SemaphoreType.DMA((frames,)),
            pltpu.SemaphoreType.DMA((peers,)),
            pltpu.SemaphoreType.DMA((peers,)),
        ],
        compiler_params=pltpu.CompilerParams(
            collective_id=0, has_side_effects=True, vmem_limit_bytes=60 * 1024 * 1024
        ),
        name="modal",
    )(counts, momentum, spread_x, table)

    parts = parts[:, :, :, :2 * per_y].reshape(4, groups * frames, share, 2, per_y, cells)
    parts = parts.transpose(4, 2, 0, 3, 1, 5).reshape(
        per_y, share, 4, 2 * groups * frames, cells
    )
    return pl.pallas_call(
        corr_kernel,
        grid=(per_y,),
        out_shape=jax.ShapeDtypeStruct((per_y, share, 2, cells, cells), jnp.float32),
        in_specs=[pl.BlockSpec((1,) + parts.shape[1:], lambda j: (j, 0, 0, 0, 0))],
        out_specs=pl.BlockSpec((1, share, 2, cells, cells), lambda j: (j, 0, 0, 0, 0)),
        compiler_params=pltpu.CompilerParams(vmem_limit_bytes=32 * 1024 * 1024),
        name="correlate",
    )(parts)


def solution(mesh):
    in_specs = (P("frames", "modes", None, None), P(), P(), P(), P(), P(), P())
    out_specs = P("modes", "frames", None, None, None)
    return jax.shard_map(
        per_device, mesh=mesh, in_specs=in_specs, out_specs=out_specs, check_vma=False
    )
```

```python
import functools
import math

import jax
import jax.numpy as jnp
from jax import lax
from jax.experimental import pallas as pl
from jax.experimental.pallas import tpu as pltpu
from jax.sharding import PartitionSpec as P

MESH = pl.DeviceIdType.MESH
ROWS = 16
CHUNK = 64
SLOTS = 3


def turned_wave(product, size, quarters):
    phase = (product + quarters * (size // 4)) % size
    return jnp.cos(phase.astype(jnp.float32) * (2.0 * math.pi / size))


def pair_counts(pair_first, pair_second, block_len):
    offsets = jnp.arange(block_len, dtype=jnp.int32)
    first_hot = pair_first[:, None, None] == offsets[None, :, None]
    second_hot = pair_second[:, None, None] == offsets[None, None, :]
    return jnp.sum((first_hot & second_hot).astype(jnp.float32), axis=0)


def modal_kernel(
    groups, half, share,
    counts_ref, m_ref, w_ref, a_ref, z_ref,
    mbuf, ghi, glo, own, partner, outgoing, relayed, onward, landed,
    m_sem, pair_send, pair_recv, relay_send, relay_recv, send_sem, recv_sem,
):
    frames, _, grid_y, cells = m_ref.shape
    rows = a_ref.shape[0] // (2 * half)
    waves = groups * share
    fr = lax.axis_index("frames")
    mode = lax.axis_index("modes")
    core = lax.rem(mode, 2)
    line = lax.div(mode, 2)
    slots = landed.shape[0]
    relay = slots != half
    peers = groups * slots
    swap = line + 1 - 2 * lax.rem(line, 2)
    far = lax.rem(line + half // 2, half)
    swap_far = lax.rem(swap + half // 2, half)
    other = (fr, line * 2 + 1 - core)
    chunks = grid_y // CHUNK

    def line_to(slot):
        if relay:
            odd = lax.rem(slot, 2)
            return odd * swap + (1 - odd) * lax.rem(line + slot, half)
        return lax.rem(line + slot, half)

    def peer_at(step):
        slot, turn = lax.div(step, groups), lax.rem(step, groups)
        return slot, lax.rem(fr + turn, groups), line_to(slot)

    barrier = pltpu.get_barrier_semaphore()

    def greet(step, carry):
        _, f, l = peer_at(step)
        pl.semaphore_signal(barrier, inc=1, device_id=(f, l * 2 + core), device_id_type=MESH)
        return carry

    def load(index):
        slot = lax.rem(index, SLOTS)
        start = pl.multiple_of(lax.rem(index, chunks) * CHUNK, CHUNK)
        return pltpu.make_async_copy(
            m_ref.at[lax.div(index, chunks), :, pl.ds(start, CHUNK), :],
            mbuf.at[slot], m_sem.at[slot],
        )

    for index in range(SLOTS - 1):
        load(jnp.int32(index)).start()
    lax.fori_loop(1, peers, greet, 0)
    pl.semaphore_signal(barrier, inc=1, device_id=other, device_id_type=MESH)
    pl.semaphore_wait(barrier, peers)

    def x_chunk(t, c, carry):
        index = t * chunks + c
        load(index).wait()

        @pl.when(index + SLOTS - 1 < frames * chunks)
        def _():
            load(index + SLOTS - 1).start()

        slot = lax.rem(index, SLOTS)
        for g in range(CHUNK // ROWS):
            block = mbuf[slot, :, g * ROWS:(g + 1) * ROWS, :]
            part = jnp.dot(
                w_ref[...], block.reshape(-1, cells), preferred_element_type=jnp.float32
            )
            high = part.astype(jnp.bfloat16)
            low = (part - high.astype(jnp.float32)).astype(jnp.bfloat16)
            at = pl.ds(pl.multiple_of(c * CHUNK + g * ROWS, ROWS), ROWS)
            ghi[:, at, :] = high.reshape(2 * waves, ROWS, cells)
            glo[:, at, :] = low.reshape(2 * waves, ROWS, cells)
        return carry

    def y_wave(t, k, carry):
        f, kk = lax.div(k, share), lax.rem(k, share)
        pair = pl.ds(2 * k, 2)
        total = jnp.dot(
            a_ref[...], ghi[pair].reshape(2 * grid_y, cells), preferred_element_type=jnp.float32
        ) + jnp.dot(
            a_ref[...], glo[pair].reshape(2 * grid_y, cells), preferred_element_type=jnp.float32
        )
        own[t, :, f, kk] = total.reshape(2, half * rows, cells).astype(jnp.bfloat16)
        return carry

    def pair_copy(t):
        return pltpu.make_async_remote_copy(
            src_ref=own.at[t, 1 - core], dst_ref=partner.at[t],
            send_sem=pair_send.at[t], recv_sem=pair_recv.at[t],
            device_id=other, device_id_type=MESH,
        )

    def spread(t):
        pair_copy(t).wait()

        def add(k, carry):
            f, kk = lax.div(k, share), lax.rem(k, share)
            total = own[t, core, f, kk].astype(jnp.float32) + partner[t, f, kk].astype(jnp.float32)
            outgoing[t, f, :, kk] = total.astype(jnp.bfloat16).reshape(half, rows, cells)
            return carry

        lax.fori_loop(0, waves, add, 0)

        if relay:
            relay_copy(t).start()
            lax.fori_loop(1, 2 * groups, functools.partial(send, t), 0)
        else:
            lax.fori_loop(1, peers, functools.partial(send, t), 0)
        landed[0, fr, t] = outgoing[t, fr, line]

    def relay_copy(t):
        return pltpu.make_async_remote_copy(
            src_ref=outgoing.at[t, :, swap_far], dst_ref=relayed.at[t],
            send_sem=relay_send.at[t], recv_sem=relay_recv.at[t],
            device_id=(fr, swap * 2 + core), device_id_type=MESH,
        )

    def send(t, step, carry):
        slot, f, l = peer_at(step)
        pltpu.make_async_remote_copy(
            src_ref=outgoing.at[t, f, l], dst_ref=landed.at[slot, fr, t],
            send_sem=send_sem.at[step], recv_sem=recv_sem.at[step],
            device_id=(f, l * 2 + core), device_id_type=MESH,
        ).start()
        return carry

    def forward(t):
        relay_copy(t).wait()

        def add(k, carry):
            f, kk = lax.div(k, share), lax.rem(k, share)
            total = outgoing[t, f, far, kk].astype(jnp.float32) + relayed[t, f, kk].astype(jnp.float32)
            onward[t, f, kk] = total.astype(jnp.bfloat16)
            return carry

        lax.fori_loop(0, waves, add, 0)

        def push(turn, carry):
            f = lax.rem(fr + turn, groups)
            at = 2 * groups + turn
            pltpu.make_async_remote_copy(
                src_ref=onward.at[t, f], dst_ref=landed.at[2, fr, t],
                send_sem=send_sem.at[at], recv_sem=recv_sem.at[at],
                device_id=(f, far * 2 + core), device_id_type=MESH,
            ).start()
            return carry

        lax.fori_loop(0, groups, push, 0)

    first, second = chunks // 8, chunks // 2

    def frame(t, carry):
        lax.fori_loop(0, first, functools.partial(x_chunk, t), 0)

        @pl.when(t > 0)
        def _():
            spread(t - 1)

        lax.fori_loop(first, second, functools.partial(x_chunk, t), 0)
        if relay:

            @pl.when(t > 0)
            def _():
                forward(t - 1)

        lax.fori_loop(second, chunks, functools.partial(x_chunk, t), 0)
        lax.fori_loop(0, waves, functools.partial(y_wave, t), 0)
        pair_copy(t).start()
        return carry

    lax.fori_loop(0, frames, frame, 0)
    spread(jnp.int32(frames - 1))
    if relay:
        forward(jnp.int32(frames - 1))

    def collect(step, carry):
        slot, f, l = peer_at(step)
        source = lax.rem(fr + groups - lax.rem(step, groups), groups)
        block = landed.at[slot, source]
        pltpu.make_async_remote_copy(
            src_ref=block, dst_ref=block,
            send_sem=send_sem.at[step], recv_sem=recv_sem.at[step],
            device_id=(f, l * 2 + core), device_id_type=MESH,
        ).wait()
        return carry

    lax.fori_loop(1, peers, collect, 0)

    def finish(index, carry):
        kk = lax.div(index, rows // ROWS)
        at = pl.ds(pl.multiple_of(lax.rem(index, rows // ROWS) * ROWS, ROWS), ROWS)
        modal = [
            [
                jnp.sum(landed[:, f, t, kk, at, :].astype(jnp.float32), axis=0)
                for t in range(frames)
            ]
            for f in range(groups)
        ]
        mean = sum(value for block in modal for value in block) / (groups * frames)
        for f in range(groups):
            centered = [value - mean for value in modal[f]]
            for b in range(frames):
                weighted = sum(counts_ref[a, b] * centered[a] for a in range(frames))
                for first, value in ((0, weighted), (2, centered[b])):
                    high = value.astype(jnp.bfloat16)
                    low = (value - high.astype(jnp.float32)).astype(jnp.bfloat16)
                    z_ref[first, f * frames + b, kk, at, :] = high
                    z_ref[first + 1, f * frames + b, kk, at, :] = low
        return carry

    lax.fori_loop(0, share * (rows // ROWS), finish, 0)


def corr_kernel(z_ref, out_ref):
    many, share, _, depth, _ = z_ref.shape
    mid = depth // 2
    for j in range(many):
        for kk in range(share):
            left = jnp.concatenate([z_ref[j, kk, 0], z_ref[j, kk, 1], z_ref[j, kk, 0]], axis=0)
            high, low = z_ref[j, kk, 2], z_ref[j, kk, 3]
            both = [
                jnp.concatenate([v, jnp.concatenate([v[mid:], -v[:mid]], axis=0)], axis=1)
                for v in (high, low)
            ]
            result = lax.dot_general(
                left, jnp.concatenate([both[0], both[0], both[1]], axis=0),
                (((0,), (0,)), ((), ())), preferred_element_type=jnp.float32,
            )
            cells = result.shape[0]
            out_ref[j, kk, 0] = result[:, :cells]
            out_ref[j, kk, 1] = result[:, cells:]


def per_device(momentum, ky_list, kx_list, ky_gain, kx_gain, pair_first, pair_second):
    frames, row_share, grid_y, cells = momentum.shape
    groups, modes = lax.axis_size("frames"), lax.axis_size("modes")
    half = modes // 2
    wave_y, wave_x = ky_list.shape[0], kx_list.shape[0]
    per_y, share = wave_y // modes, wave_x // groups
    rows = -(-2 * per_y // ROWS) * ROWS
    grid_x = row_share * modes

    def by_owner(values):
        values = values.reshape(half, 2, 1, per_y).transpose(1, 0, 2, 3)
        values = jnp.broadcast_to(values, (2, half, 2, per_y)).reshape(2, half, 2 * per_y)
        return jnp.pad(values, ((0, 0), (0, 0), (0, rows - 2 * per_y))).reshape(-1, 1)

    shape = (2 * half * rows, 2 * grid_y)
    row = lax.broadcasted_iota(jnp.int32, shape, 0) % rows
    column = lax.broadcasted_iota(jnp.int32, shape, 1)
    quarters = (row >= per_y).astype(jnp.int32) + (column >= grid_y).astype(jnp.int32)
    table = turned_wave(by_owner(ky_list) * (column % grid_y), grid_y, quarters)
    table = (table * (by_owner(ky_gain) / math.sqrt(grid_y))).astype(jnp.bfloat16)

    shape = (2 * wave_x * ROWS, row_share * ROWS)
    row = lax.broadcasted_iota(jnp.int32, shape, 0)
    column = lax.broadcasted_iota(jnp.int32, shape, 1)
    x_index = lax.axis_index("modes") * row_share + column // ROWS
    kx_rows = jnp.repeat(kx_list, 2 * ROWS)[:, None]
    kx_scale = jnp.repeat(kx_gain, 2 * ROWS)[:, None] / math.sqrt(grid_x)
    spread_x = turned_wave(kx_rows * x_index, grid_x, row // ROWS % 2 * 3) * kx_scale
    spread_x = jnp.where(row % ROWS == column % ROWS, spread_x, 0.0).astype(jnp.bfloat16)
    counts = pair_counts(pair_first, pair_second, frames) / pair_first.shape[0]

    bf16 = jnp.bfloat16
    vmem = pl.BlockSpec(memory_space=pltpu.VMEM)
    slots = 3 if half == 4 else half
    peers = groups * slots
    parts = pl.pallas_call(
        functools.partial(modal_kernel, groups, half, share),
        out_shape=jax.ShapeDtypeStruct((4, groups * frames, share, rows, cells), bf16),
        in_specs=[
            pl.BlockSpec(memory_space=pltpu.SMEM),
            pl.BlockSpec(memory_space=pl.ANY),
            vmem,
            vmem,
        ],
        out_specs=vmem,
        scratch_shapes=[
            pltpu.VMEM((SLOTS, row_share, CHUNK, cells), bf16),
            pltpu.VMEM((2 * wave_x, grid_y, cells), bf16),
            pltpu.VMEM((2 * wave_x, grid_y, cells), bf16),
            pltpu.VMEM((frames, 2, groups, share, half * rows, cells), bf16),
            pltpu.VMEM((frames, groups, share, half * rows, cells), bf16),
            pltpu.VMEM((frames, groups, half, share, rows, cells), bf16),
            pltpu.VMEM((frames, groups, share, rows, cells), bf16),
            pltpu.VMEM((frames, groups, share, rows, cells), bf16),
            pltpu.VMEM((slots, groups, frames, share, rows, cells), bf16),
            pltpu.SemaphoreType.DMA((SLOTS,)),
            pltpu.SemaphoreType.DMA((frames,)),
            pltpu.SemaphoreType.DMA((frames,)),
            pltpu.SemaphoreType.DMA((frames,)),
            pltpu.SemaphoreType.DMA((frames,)),
            pltpu.SemaphoreType.DMA((peers,)),
            pltpu.SemaphoreType.DMA((peers,)),
        ],
        compiler_params=pltpu.CompilerParams(
            collective_id=0, has_side_effects=True, vmem_limit_bytes=60 * 1024 * 1024
        ),
        name="modal",
    )(counts, momentum, spread_x, table)

    parts = parts[:, :, :, :2 * per_y].reshape(4, groups * frames, share, 2, per_y, cells)
    parts = parts.transpose(4, 2, 0, 3, 1, 5).reshape(
        per_y, share, 4, 2 * groups * frames, cells
    )
    many = 3 if per_y % 3 == 0 else 1
    return pl.pallas_call(
        corr_kernel,
        grid=(per_y // many,),
        out_shape=jax.ShapeDtypeStruct((per_y, share, 2, cells, cells), jnp.float32),
        in_specs=[pl.BlockSpec((many,) + parts.shape[1:], lambda j: (j, 0, 0, 0, 0))],
        out_specs=pl.BlockSpec((many, share, 2, cells, cells), lambda j: (j, 0, 0, 0, 0)),
        compiler_params=pltpu.CompilerParams(vmem_limit_bytes=32 * 1024 * 1024),
        name="correlate",
    )(parts)


def solution(mesh):
    in_specs = (P("frames", "modes", None, None), P(), P(), P(), P(), P(), P())
    out_specs = P("modes", "frames", None, None, None)
    return jax.shard_map(
        per_device, mesh=mesh, in_specs=in_specs, out_specs=out_specs, check_vma=False
    )
```
